512 devices in a mesh: row: 16 (over x, z_hi), col: 32 (over z_lo, y, core).
Axes of the slice: x: 4, y: 8, z: 8 (z_hi: 4, z_lo: 2; z = z_hi * 2 + z_lo), core: 2. Of those that a mesh axis runs over, the one named last changes fastest.
Arguments:
- activations: bfloat16 [16384, 768], P('row', 'col'), may hold values from -6 to 6
- partner: int32 [64], replicated, may hold values from 0 to 63, each once
- mix_weight: int32 [64], replicated, may hold values from 0 to 256
- weight: bfloat16 [768, 24576], P(None, 'col'), may hold values from -0.15625 to 0.15625
- bias: float32 [24576], P('col'), may hold values from -3 to 3
- earlier: bfloat16 [16384, 24576], P('row', 'col'), may hold values from -5 to 5
- cotangent: bfloat16 [16384, 24576], P('row', 'col'), may hold values from -6 to 6
Outputs:
- hidden: bfloat16 [16384, 24576], P('row', 'col')
- weight_grad: float32 [768, 24576], P('row', 'col')
The draws below stay inside these ranges and needn't reach their ends.
Inputs may be any that keep to these rules, and one draw needn't show every extreme that they name: `partner`: each image is named exactly once.
All inputs are finite; a program needn't handle non-finite values.
Results may differ from the reference program's by a relative error of at most 0.015.
Values may be sent and summed in bfloat16 or wider, within the bound.
A program may use at most 64 MiB of HBM per device.

```python
import jax
import jax.numpy as jnp
from jax import lax

FF = 24576
PATCHES = 256
KWIN = 768
IMAGES = 64
TOK_DEV = 1024
TOKENS = 16384
N_ROW = 16


def place_ends(array, own_key, least, high):
    dims = array.shape
    index_at = [jax.random.randint(jax.random.fold_in(own_key, axis), (), 0, dims[axis]) for axis in range(len(dims))]
    array = array.at[tuple(index_at)].set(least)
    longest = dims.index(max(dims))
    index_at[longest] = (index_at[longest] + 1) % dims[longest]
    return array.at[tuple(index_at)].set(high)


def shard_levels(own_key, dims, pieces, least, top_value):
    level, own = 1.0, jax.random.fold_in(own_key, 6)
    for dim, parts in pieces:
        steps = jnp.exp(jax.random.uniform(jax.random.fold_in(own, dim), (parts,), jnp.float32, least / len(pieces), top_value / len(pieces)))
        level = level * jnp.repeat(steps, dims[dim] // parts).reshape([-1 if axis == dim else 1 for axis in range(len(dims))])
    return level


def normal_values(rng, dims, scale, limit, shards=(), kind=jnp.bfloat16):
    array = scale * jax.random.normal(rng, dims, jnp.float32)
    if shards:
        array = array * shard_levels(rng, dims, shards, -0.22, 0.18)
    return jnp.clip(array, -limit, limit).astype(kind)


def setup_inputs(seed: int = 0) -> dict:
    keys = jax.random.split(jax.random.key(seed), 8)
    activations = normal_values(keys[0], (TOKENS, KWIN), 1.0, 6.0, ((0, 16), (1, 32)))
    partner = jax.random.permutation(keys[1], IMAGES).astype(jnp.int32)
    mix_weight = place_ends(jax.random.randint(keys[2], (IMAGES,), 0, 257), jax.random.fold_in(keys[2], 1), 0, 256).astype(jnp.int32)
    weight = normal_values(keys[3], (KWIN, FF), (2 * KWIN) ** -0.5, 0.15625, ((1, 32),))
    bias = normal_values(keys[4], (FF,), 0.5, 3.0, ((0, 32),), jnp.float32)
    earlier = normal_values(keys[5], (TOKENS, FF), 0.7, 5.0, ((0, 16), (1, 32)))
    cotangent = normal_values(keys[6], (TOKENS, FF), 1.0, 6.0, ((0, 16), (1, 32)))
    return dict(activations=activations, partner=partner, mix_weight=mix_weight, weight=weight, bias=bias, earlier=earlier, cotangent=cotangent)


def slope(preact):
    normal_cdf = 0.5 * (1.0 + lax.erf(preact * 0.7071067811865476))
    density = jnp.exp(-0.5 * preact * preact) * 0.3989422804014327
    return normal_cdf + preact * density


def reference(activations, partner, mix_weight, weight, bias, earlier, cotangent):
    width = activations.shape[1]
    images = activations.reshape(IMAGES, PATCHES, width)
    other = images[partner]
    share = (mix_weight.astype(jnp.float32) / 256.0)[:, None, None]
    blended = (share * images.astype(jnp.float32) + (1.0 - share) * other.astype(jnp.float32)).astype(jnp.bfloat16)
    blended = blended.reshape(TOKENS, width)
    product = jnp.dot(blended, weight, preferred_element_type=jnp.float32)
    preact = earlier.astype(jnp.float32) + product + bias[None, :]
    normal_cdf = 0.5 * (1.0 + lax.erf(preact * 0.7071067811865476))
    hidden = (preact * normal_cdf).astype(jnp.bfloat16)
    grad_pre = (cotangent.astype(jnp.float32) * slope(preact)).astype(jnp.bfloat16)
    block_b = blended.reshape(N_ROW, TOK_DEV, width)
    block_g = grad_pre.reshape(N_ROW, TOK_DEV, grad_pre.shape[1])

    def add_block(carry, pair):
        term = jnp.dot(pair[0].T, pair[1], preferred_element_type=jnp.float32)
        return carry + term.astype(jnp.bfloat16).astype(jnp.float32), None

    start_sum = jnp.zeros((width, grad_pre.shape[1]), jnp.float32)
    weight_grad, unused = lax.scan(add_block, start_sum, (block_b, block_g))
    return hidden, weight_grad
```

```python
import jax
import jax.numpy as jnp
from jax import lax
from jax.experimental import pallas as pl
from jax.experimental.pallas import tpu as pltpu
from jax.sharding import PartitionSpec as P

X, Z_HI, Z_LO, Y = 4, 4, 2, 8
CHIPS = Z_LO * Y
PATCHES = 256
HALF = 512
TOK = 1024
K_DEV, K_CHIP, K_ALL = 24, 48, 768
FF_DEV, FB = 768, 256
NF = FF_DEV // FB
X_ROWS, OUT_ROWS = K_ALL // X, K_ALL // (X * Z_HI)
TILE = 256
HOPS = Y // 2


def kernel(
    partner, mix, act, weight_in, bias, earlier_in, cot_in,
    hidden_out, grad_out,
    ax, images, own, sel, cand, ball, blend_t, weight, earlier, cot, hidden, grad, term, rx, zs, rz,
    send_a, recv_a, send_p, recv_p, send_z, recv_z, send_y, recv_y, send_s, recv_s,
    send_rx, recv_rx, send_rz, recv_rz, local_a, local_in, local_out,
):
    row, col = lax.axis_index("row"), lax.axis_index("col")
    x, zh = lax.div(row, Z_HI), lax.rem(row, Z_HI)
    chip, core = lax.div(col, 2), lax.rem(col, 2)
    zl, y = lax.div(chip, Y), lax.rem(chip, Y)
    other_core = 1 - core
    f32, bf16 = jnp.float32, jnp.bfloat16

    def device(dx=0, dz=0, dl=0, dy=0, dh=0):
        r = lax.rem(x + dx, X) * Z_HI + lax.rem(zh + dz, Z_HI)
        c = (lax.rem(zl + dl, Z_LO) * Y + lax.rem(y + dy, Y)) * 2 + lax.rem(core + dh, 2)
        return {"row": r, "col": c}

    def remote(src, dst, send, recv, to):
        return pltpu.make_async_remote_copy(
            src_ref=src, dst_ref=dst, send_sem=send, recv_sem=recv,
            device_id=to, device_id_type=pl.DeviceIdType.MESH,
        )

    loads = [
        pltpu.make_async_copy(weight_in, weight, local_in.at[0]),
        pltpu.make_async_copy(earlier_in, earlier, local_in.at[1]),
        pltpu.make_async_copy(cot_in, cot, local_in.at[2]),
    ]
    mine = [
        pltpu.make_async_copy(act, ax.at[x], local_a.at[0]),
        pltpu.make_async_copy(act.at[:, pl.ds(pl.multiple_of(core * HALF, HALF), HALF)], own.at[0], local_a.at[1]),
    ]
    for copy in mine:
        copy.start()

    barrier = pltpu.get_barrier_semaphore()
    peers = [device(dx=d) for d in range(1, X)]
    peers += [device(dz=d, dh=h) for d in range(Z_HI) for h in range(2) if d or h]
    peers += [device(dl=1), device(dy=1), device(dy=Y - 1)]
    for peer in peers:
        pl.semaphore_signal(barrier, inc=1, device_id=peer, device_id_type=pl.DeviceIdType.MESH)
    pl.semaphore_wait(barrier, len(peers))

    first = [remote(act, ax.at[x], send_a.at[d], recv_a.at[d], device(dx=d)) for d in (2, 1, 3)]
    first.append(
        remote(
            act.at[:, pl.ds(pl.multiple_of(other_core * HALF, HALF), HALF)],
            own.at[1], send_a.at[0], recv_a.at[0], device(dh=1),
        )
    )
    for copy in first:
        copy.start()
    for copy in loads:
        copy.start()
    mine[0].wait()
    for copy in first[:3]:
        copy.wait_recv()
    for i in range(X):
        for j in range(4):
            images[i * 4 + j] = ax[i, :, j * PATCHES : (j + 1) * PATCHES]

    second = []
    for d, h in ((2, 0), (2, 1), (1, 0), (1, 1), (3, 0), (3, 1), (0, 1), (0, 0)):
        to_row = x * Z_HI + lax.rem(zh + d, Z_HI)
        to_core = lax.rem(core + h, 2)
        for i in range(2):
            image = partner[to_row * 4 + to_core * 2 + i]
            value = images[lax.div(image, 16) * 4 + lax.rem(image, 4)]
            span = slice(i * PATCHES, (i + 1) * PATCHES)
            if d or h:
                sel[d, h, :, span] = value
            else:
                cand[0, 0, :, span] = value
        if d or h:
            copy = remote(sel.at[d, h], cand.at[d, h], send_p.at[d, h], recv_p.at[d, h], device(dz=d, dh=h))
            copy.start()
            second.append(copy)
    mine[1].wait()
    first[3].wait_recv()
    for copy in second:
        copy.wait_recv()

    for i in range(2):
        image = row * 4 + core * 2 + i
        source = lax.rem(lax.div(partner[image], 4), Z_HI)
        slot = lax.rem(zh - source + Z_HI, Z_HI)
        share = mix[image].astype(f32) / 256.0
        span = slice(i * PATCHES, (i + 1) * PATCHES)
        parts = []
        for k in range(2):
            rel = lax.rem(core + k, 2)
            parts.append(share * own[rel, :, span].astype(f32) + (1.0 - share) * cand[slot, rel, :, span].astype(f32))
        ball[core, chip, :, span] = jnp.concatenate(parts, axis=0).astype(bf16)

    def place(b, dy):
        return ball.at[core, lax.rem(zl + b, Z_LO) * Y + lax.rem(y + dy, Y)]

    pending = []
    across = remote(place(0, 0), place(0, 0), send_z, recv_z, device(dl=1))
    across.start()
    pending.append(across)

    def ring(way, b, hop):
        step = 1 if way == 0 else Y - 1
        block = place(b, (Y - step) * (hop - 1) % Y)
        return remote(block, block, send_y.at[way, b, hop - 1], recv_y.at[way, b, hop - 1], device(dy=step))

    def to_sibling(b, dy):
        block = place(b, dy)
        return remote(block, block, send_s.at[b, dy], recv_s.at[b, dy], device(dh=1))

    def start(copy):
        copy.start()
        pending.append(copy)
        return copy

    rings = {}
    siblings = []
    for way in range(2):
        rings[way, 0, 1] = start(ring(way, 0, 1))
    siblings.append(start(to_sibling(0, 0)))
    across.wait_recv()
    for way in range(2):
        rings[way, 1, 1] = start(ring(way, 1, 1))
    siblings.append(start(to_sibling(1, 0)))

    def last_hop(way, b):
        return HOPS if way == b else HOPS - 1

    for hop in range(1, HOPS + 1):
        for b in range(2):
            for way in range(2):
                if hop > last_hop(way, b):
                    continue
                rings[way, b, hop].wait_recv()
                if hop < last_hop(way, b):
                    rings[way, b, hop + 1] = start(ring(way, b, hop + 1))
                siblings.append(start(to_sibling(b, (hop if way else Y - hop) % Y)))
    for copy in siblings:
        copy.wait_recv()

    def flip(t, carry):
        at = pl.ds(pl.multiple_of(t * 128, 128), 128)
        for h in range(2):
            rows = pl.ds(pl.multiple_of(h * HALF + t * 128, 128), 128)
            for b in range(Z_LO):
                block = ball[h, b * Y : (b + 1) * Y, :, at].reshape(Y * K_CHIP, 128)
                blend_t[rows, b * Y * K_CHIP : (b + 1) * Y * K_CHIP] = block.T
        return carry

    lax.fori_loop(0, HALF // 128, flip, 0)
    for copy in loads:
        copy.wait()

    writes, sums = [], []
    for f in range(NF):
        cols = slice(f * FB, (f + 1) * FB)

        def forward(t, carry, cols=cols):
            rows = pl.ds(pl.multiple_of(t * TILE, TILE), TILE)
            product = jnp.dot(blend_t[rows, :], weight[:, cols], preferred_element_type=f32)
            preact = earlier[rows, cols].astype(f32) + product + bias[:, cols]
            normal_cdf = 0.5 * (1.0 + lax.erf(preact * 0.7071067811865476))
            density = jnp.exp(-0.5 * preact * preact) * 0.3989422804014327
            hidden[rows, cols] = (preact * normal_cdf).astype(bf16)
            grad[rows, :] = (cot[rows, cols].astype(f32) * (normal_cdf + preact * density)).astype(bf16)
            return carry

        lax.fori_loop(0, TOK // TILE, forward, 0)
        write = pltpu.make_async_copy(hidden.at[:, cols], hidden_out.at[:, cols], local_out.at[f])
        write.start()
        writes.append(write)
        out = []
        for d in (2, 1, 3, 0):
            to_x = lax.rem(x + d, X)
            chips = pl.ds(to_x * (CHIPS // X), CHIPS // X)
            total = jnp.dot(
                ball[0, chips].reshape(X_ROWS, HALF), grad[:HALF, :], preferred_element_type=f32
            ) + jnp.dot(ball[1, chips].reshape(X_ROWS, HALF), grad[HALF:, :], preferred_element_type=f32)
            term[f, d] = total.astype(bf16)
            if d:
                out.append(start(remote(term.at[f, d], rx.at[f, d - 1], send_rx.at[f, d - 1], recv_rx.at[f, d - 1], device(dx=d))))
        sums.append(out)

    ends = []
    for f in range(NF):
        for copy in sums[f]:
            copy.wait_recv()
        for q in range(Z_HI):
            rows = slice(q * OUT_ROWS, (q + 1) * OUT_ROWS)
            total = term[f, 0, rows, :].astype(f32)
            for d in range(1, X):
                total = total + rx[f, d - 1, rows, :].astype(f32)
            zs[f, q] = total.astype(bf16)
        out = []
        for d in (2, 1, 3):
            out.append(
                start(remote(zs.at[f, lax.rem(zh + d, Z_HI)], rz.at[f, d - 1], send_rz.at[f, d - 1], recv_rz.at[f, d - 1], device(dz=d)))
            )
        ends.append(out)
    for f in range(NF):
        for copy in ends[f]:
            copy.wait_recv()
        total = zs[f, zh].astype(f32)
        for d in range(1, Z_HI):
            total = total + rz[f, d - 1].astype(f32)
        grad_out[:, f * FB : (f + 1) * FB] = total

    for copy in first + second + pending:
        copy.wait_send()
    for copy in writes:
        copy.wait()


def local(activations, partner, mix_weight, weight, bias, earlier, cotangent):
    bf16, dma = jnp.bfloat16, pltpu.SemaphoreType.DMA
    hbm, vmem, smem = (pl.BlockSpec(memory_space=s) for s in (pl.ANY, pltpu.VMEM, pltpu.SMEM))
    return pl.pallas_call(
        kernel,
        out_shape=(
            jax.ShapeDtypeStruct((TOK, FF_DEV), bf16),
            jax.ShapeDtypeStruct((OUT_ROWS, FF_DEV), jnp.float32),
        ),
        in_specs=[smem, smem, hbm, hbm, vmem, hbm, hbm],
        out_specs=(hbm, vmem),
        scratch_shapes=[
            pltpu.VMEM((X, K_DEV, TOK), bf16),
            pltpu.VMEM((X * 4, K_DEV, PATCHES), bf16),
            pltpu.VMEM((2, K_DEV, HALF), bf16),
            pltpu.VMEM((Z_HI, 2, K_DEV, HALF), bf16),
            pltpu.VMEM((Z_HI, 2, K_DEV, HALF), bf16),
            pltpu.VMEM((2, CHIPS, K_CHIP, HALF), bf16),
            pltpu.VMEM((TOK, K_ALL), bf16),
            pltpu.VMEM((K_ALL, FF_DEV), bf16),
            pltpu.VMEM((TOK, FF_DEV), bf16),
            pltpu.VMEM((TOK, FF_DEV), bf16),
            pltpu.VMEM((TOK, FF_DEV), bf16),
            pltpu.VMEM((TOK, FB), bf16),
            pltpu.VMEM((NF, X, X_ROWS, FB), bf16),
            pltpu.VMEM((NF, X - 1, X_ROWS, FB), bf16),
            pltpu.VMEM((NF, Z_HI, OUT_ROWS, FB), bf16),
            pltpu.VMEM((NF, Z_HI - 1, OUT_ROWS, FB), bf16),
            dma((X,)), dma((X,)),
            dma((Z_HI, 2)), dma((Z_HI, 2)),
            dma, dma,
            dma((2, 2, HOPS)), dma((2, 2, HOPS)),
            dma((2, Y)), dma((2, Y)),
            dma((NF, X - 1)), dma((NF, X - 1)),
            dma((NF, Z_HI - 1)), dma((NF, Z_HI - 1)),
            dma((2,)), dma((3,)), dma((NF,)),
        ],
        compiler_params=pltpu.CompilerParams(
            collective_id=0, has_side_effects=True, vmem_limit_bytes=56 * 2**20
        ),
    )(partner, mix_weight, activations.T, weight, bias.reshape(1, FF_DEV), earlier, cotangent)


def solution(mesh):
    return jax.shard_map(
        local,
        mesh=mesh,
        in_specs=(P("row", "col"), P(), P(), P(None, "col"), P("col"), P("row", "col"), P("row", "col")),
        out_specs=(P("row", "col"), P("row", "col")),
        check_vma=False,
    )
```

```python
import jax
import jax.numpy as jnp
from jax import lax
from jax.experimental import pallas as pl
from jax.experimental.pallas import tpu as pltpu
from jax.sharding import PartitionSpec as P

X, Z_HI, Z_LO, Y = 4, 4, 2, 8
CHIPS = Z_LO * Y
PATCHES = 256
HALF = 512
TOK = 1024
K_DEV, K_CHIP, K_ALL = 24, 48, 768
FF_DEV, FB = 768, 256
NF = FF_DEV // FB
X_ROWS, OUT_ROWS = K_ALL // X, K_ALL // (X * Z_HI)
TILE = 256


def kernel(
    partner, mix, act, weight_in, bias_in, earlier_in, cot_in,
    hidden, grad_out,
    ax, images, own, sel, cand, ball, blend_t, weight, bias, earlier, cot, grad, zterm, zin, term, rx, zs, rz,
    send_a, recv_a, send_p, recv_p, send_y, recv_y, send_l, recv_l, send_d, send_s, recv_s,
    send_rx, recv_rx, send_rz, recv_rz, local_a, local_in,
):
    row, col = lax.axis_index("row"), lax.axis_index("col")
    x, zh = lax.div(row, Z_HI), lax.rem(row, Z_HI)
    chip, core = lax.div(col, 2), lax.rem(col, 2)
    zl, y = lax.div(chip, Y), lax.rem(chip, Y)
    other_core = 1 - core
    f32, bf16 = jnp.float32, jnp.bfloat16

    def device(dx=0, dz=0, dl=0, dy=0, dh=0):
        r = lax.rem(x + dx, X) * Z_HI + lax.rem(zh + dz, Z_HI)
        c = (lax.rem(zl + dl, Z_LO) * Y + lax.rem(y + dy, Y)) * 2 + lax.rem(core + dh, 2)
        return {"row": r, "col": c}

    def remote(src, dst, send, recv, to):
        return pltpu.make_async_remote_copy(
            src_ref=src, dst_ref=dst, send_sem=send, recv_sem=recv,
            device_id=to, device_id_type=pl.DeviceIdType.MESH,
        )

    loads = [
        pltpu.make_async_copy(weight_in, weight, local_in.at[0]),
        pltpu.make_async_copy(bias_in, bias, local_in.at[3]),
        pltpu.make_async_copy(earlier_in, earlier, local_in.at[1]),
        pltpu.make_async_copy(cot_in, cot, local_in.at[2]),
    ]
    mine = [
        pltpu.make_async_copy(act, ax.at[x], local_a.at[0]),
        pltpu.make_async_copy(act.at[:, pl.ds(pl.multiple_of(core * HALF, HALF), HALF)], own.at[0], local_a.at[1]),
    ]
    for copy in mine:
        copy.start()

    barrier = pltpu.get_barrier_semaphore()
    peers = [device(dx=d) for d in range(1, X)]
    peers += [device(dz=d, dh=h) for d in range(Z_HI) for h in range(2) if d or h]
    peers += [device(dl=1)] + [device(dl=l, dy=d) for l in range(Z_LO) for d in (1, 2, Y - 2, Y - 1)]
    for peer in peers:
        pl.semaphore_signal(barrier, inc=1, device_id=peer, device_id_type=pl.DeviceIdType.MESH)
    pl.semaphore_wait(barrier, len(peers))

    first = [remote(act, ax.at[x], send_a.at[d], recv_a.at[d], device(dx=d)) for d in (2, 1, 3)]
    first.append(
        remote(
            act.at[:, pl.ds(pl.multiple_of(other_core * HALF, HALF), HALF)],
            own.at[1], send_a.at[0], recv_a.at[0], device(dh=1),
        )
    )
    for copy in first:
        copy.start()
    for copy in loads:
        copy.start()
    mine[0].wait()
    for copy in first[:3]:
        copy.wait_recv()
    for i in range(X):
        for j in range(4):
            images[i * 4 + j] = ax[i, :, j * PATCHES : (j + 1) * PATCHES]

    second = []
    for d, h in ((2, 0), (2, 1), (1, 0), (1, 1), (3, 0), (3, 1), (0, 1), (0, 0)):
        to_row = x * Z_HI + lax.rem(zh + d, Z_HI)
        to_core = lax.rem(core + h, 2)
        for i in range(2):
            image = partner[to_row * 4 + to_core * 2 + i]
            value = images[lax.div(image, 16) * 4 + lax.rem(image, 4)]
            span = slice(i * PATCHES, (i + 1) * PATCHES)
            if d or h:
                sel[d, h, :, span] = value
            else:
                cand[0, 0, :, span] = value
        if d or h:
            copy = remote(sel.at[d, h], cand.at[d, h], send_p.at[d, h], recv_p.at[d, h], device(dz=d, dh=h))
            copy.start()
            second.append(copy)
    mine[1].wait()
    first[3].wait_recv()
    for copy in second:
        copy.wait_recv()

    for i in range(2):
        image = row * 4 + core * 2 + i
        source = lax.rem(lax.div(partner[image], 4), Z_HI)
        slot = lax.rem(zh - source + Z_HI, Z_HI)
        share = mix[image].astype(f32) / 256.0
        span = slice(i * PATCHES, (i + 1) * PATCHES)
        parts = []
        for k in range(2):
            rel = lax.rem(core + k, 2)
            parts.append(share * own[rel, :, span].astype(f32) + (1.0 - share) * cand[slot, rel, :, span].astype(f32))
        ball[core, chip, :, span] = jnp.concatenate(parts, axis=0).astype(bf16)

    pending = []

    def start(copy):
        copy.start()
        pending.append(copy)
        return copy

    def place(plane, dy):
        return ball.at[core, lax.rem(zl + plane, Z_LO) * Y + lax.rem(y + dy, Y)]

    def along_y(off, step, at=None):
        block, at = place(0, off), (off - step) % Y if at is None else at
        start(remote(block, block, send_y.at[at], recv_y.at[at], device(dy=step)))

    def aslant(off, step, at):
        block = place(0, off)
        start(remote(block, block, send_d.at[at], recv_l.at[at], device(dl=1, dy=step)))

    def to_sibling(plane, off):
        block = place(plane, off)
        start(remote(block, block, send_s.at[plane, off], recv_s.at[plane, off], device(dh=1)))

    def spread(off):
        block = place(0, off)
        start(remote(block, block, send_l.at[off], recv_l.at[off], device(dl=1)))
        to_sibling(0, off)

    def arrival(recv, plane, off):
        block = place(plane, off)
        pltpu.make_async_copy(block, block, recv.at[off]).wait()

    along_y(0, 2)
    along_y(0, 6)
    along_y(0, 1)
    along_y(0, 7)
    spread(0)
    for off in (7, 1):
        arrival(recv_y, 0, off)
        spread(off)
    for off in (6, 2):
        arrival(recv_y, 0, off)
    half_way, onward = 6 - 4 * core, 2 + 4 * core
    along_y(half_way, onward, 4)
    aslant(half_way, onward, 4)
    for off, step in ((6, 1), (2, 7)):
        along_y(off, step)
        aslant(off, step, (off - step) % Y)
    for off in (6, 2):
        spread(off)
    for off in (0, 7, 1, 6, 2):
        arrival(recv_l, 1, off)
        to_sibling(1, off)
    for off in (5, 3, 4):
        arrival(recv_y, 0, off)
        to_sibling(0, off)
    for off in (5, 3, 4):
        arrival(recv_l, 1, off)
        to_sibling(1, off)
    for plane in range(Z_LO):
        for off in range(Y):
            block = ball.at[other_core, lax.rem(zl + plane, Z_LO) * Y + lax.rem(y + off, Y)]
            pltpu.make_async_copy(block, block, recv_s.at[plane, off]).wait()

    def flip(t, carry):
        at = pl.ds(pl.multiple_of(t * 128, 128), 128)
        for h in range(2):
            rows = pl.ds(pl.multiple_of(h * HALF + t * 128, 128), 128)
            for b in range(Z_LO):
                block = ball[h, b * Y : (b + 1) * Y, :, at].reshape(Y * K_CHIP, 128)
                blend_t[rows, b * Y * K_CHIP : (b + 1) * Y * K_CHIP] = block.T
        return carry

    lax.fori_loop(0, HALF // 128, flip, 0)
    for copy in loads:
        copy.wait()

    def forward(f):
        cols = slice(f * FB, (f + 1) * FB)
        for t in range(TOK // TILE):
            rows = slice(t * TILE, (t + 1) * TILE)
            product = jnp.dot(blend_t[rows, :], weight[:, cols], preferred_element_type=f32)
            preact = earlier[rows, cols].astype(f32) + product + bias[cols]
            normal_cdf = 0.5 * (1.0 + lax.erf(preact * 0.7071067811865476))
            density = jnp.exp(-0.5 * preact * preact) * 0.3989422804014327
            hidden[rows, cols] = (preact * normal_cdf).astype(bf16)
            grad[rows, :] = (cot[rows, cols].astype(f32) * (normal_cdf + preact * density)).astype(bf16)

    def terms(to_x):
        chips = pl.ds(to_x * (CHIPS // X), CHIPS // X)
        return jnp.dot(
            ball[0, chips].reshape(X_ROWS, HALF), grad[:HALF, :], preferred_element_type=f32
        ) + jnp.dot(ball[1, chips].reshape(X_ROWS, HALF), grad[HALF:, :], preferred_element_type=f32)

    def over_x(f, d, src, dst):
        return start(remote(src, dst, send_rx.at[f, d - 1], recv_rx.at[f, d - 1], device(dx=d)))

    def over_z(f, d, src, dst):
        return start(remote(src, dst, send_rz.at[f, d - 1], recv_rz.at[f, d - 1], device(dz=d)))

    forward(0)
    for to_x in range(X):
        total = terms(to_x).astype(bf16)
        for q in range(Z_HI):
            zterm[q, to_x] = total[q * OUT_ROWS : (q + 1) * OUT_ROWS, :]
    begun = {0: [over_z(0, d, zterm.at[lax.rem(zh + d, Z_HI)], zin.at[d - 1]) for d in (2, 1, 3)]}
    for f in range(1, NF):
        forward(f)
        begun[f] = []
        for d in (2, 1, 3, 0):
            term[f - 1, d] = terms(lax.rem(x + d, X)).astype(bf16)
            if d:
                begun[f].append(over_x(f, d, term.at[f - 1, d], rx.at[f - 1, d - 1]))

    ends = {}
    for f in range(NF):
        for copy in begun[f]:
            copy.wait_recv()
        if f == 0:
            for to_x in range(X):
                total = zterm[zh, to_x].astype(f32)
                for d in range(1, Z_HI):
                    total = total + zin[d - 1, to_x].astype(f32)
                zs[0, to_x] = total.astype(bf16)
            ends[f] = [over_x(0, d, zs.at[0, lax.rem(x + d, X)], rz.at[0, d - 1]) for d in (2, 1, 3)]
        else:
            for q in range(Z_HI):
                rows = slice(q * OUT_ROWS, (q + 1) * OUT_ROWS)
                total = term[f - 1, 0, rows, :].astype(f32)
                for d in range(1, X):
                    total = total + rx[f - 1, d - 1, rows, :].astype(f32)
                zs[f, q] = total.astype(bf16)
            ends[f] = [over_z(f, d, zs.at[f, lax.rem(zh + d, Z_HI)], rz.at[f, d - 1]) for d in (2, 1, 3)]
    for f in range(NF):
        for copy in ends[f]:
            copy.wait_recv()
        total = zs[f, zh if f else x].astype(f32)
        for d in range(1, Z_HI):
            total = total + rz[f, d - 1].astype(f32)
        grad_out[:, f * FB : (f + 1) * FB] = total

    for copy in first + second + pending:
        copy.wait_send()


def local(activations, partner, mix_weight, weight, bias, earlier, cotangent):
    bf16, dma = jnp.bfloat16, pltpu.SemaphoreType.DMA
    hbm, vmem, smem = (pl.BlockSpec(memory_space=s) for s in (pl.ANY, pltpu.VMEM, pltpu.SMEM))
    return pl.pallas_call(
        kernel,
        out_shape=(
            pltpu.VMEM((TOK, FF_DEV), bf16),
            pltpu.VMEM((OUT_ROWS, FF_DEV), jnp.float32),
        ),
        in_specs=[smem, smem, hbm, hbm, hbm, hbm, hbm],
        out_specs=(vmem, vmem),
        scratch_shapes=[
            pltpu.VMEM((X, K_DEV, TOK), bf16),
            pltpu.VMEM((X * 4, K_DEV, PATCHES), bf16),
            pltpu.VMEM((2, K_DEV, HALF), bf16),
            pltpu.VMEM((Z_HI, 2, K_DEV, HALF), bf16),
            pltpu.VMEM((Z_HI, 2, K_DEV, HALF), bf16),
            pltpu.VMEM((2, CHIPS, K_CHIP, HALF), bf16),
            pltpu.VMEM((TOK, K_ALL), bf16),
            pltpu.VMEM((K_ALL, FF_DEV), bf16),
            pltpu.VMEM((FF_DEV,), jnp.float32),
            pltpu.VMEM((TOK, FF_DEV), bf16),
            pltpu.VMEM((TOK, FF_DEV), bf16),
            pltpu.VMEM((TOK, FB), bf16),
            pltpu.VMEM((Z_HI, X, OUT_ROWS, FB), bf16),
            pltpu.VMEM((Z_HI - 1, X, OUT_ROWS, FB), bf16),
            pltpu.VMEM((NF - 1, X, X_ROWS, FB), bf16),
            pltpu.VMEM((NF - 1, X - 1, X_ROWS, FB), bf16),
            pltpu.VMEM((NF, Z_HI, OUT_ROWS, FB), bf16),
            pltpu.VMEM((NF, Z_HI - 1, OUT_ROWS, FB), bf16),
            dma((X,)), dma((X,)),
            dma((Z_HI, 2)), dma((Z_HI, 2)),
            dma((Y,)), dma((Y,)), dma((Y,)), dma((Y,)), dma((Y,)),
            dma((2, Y)), dma((2, Y)),
            dma((NF, X - 1)), dma((NF, X - 1)),
            dma((NF, Z_HI - 1)), dma((NF, Z_HI - 1)),
            dma((2,)), dma((4,)),
        ],
        compiler_params=pltpu.CompilerParams(
            collective_id=0, has_side_effects=True, vmem_limit_bytes=56 * 2**20
        ),
    )(partner, mix_weight, activations.T, weight, bias, earlier, cotangent)


def solution(mesh):
    return jax.shard_map(
        local,
        mesh=mesh,
        in_specs=(P("row", "col"), P(), P(), P(None, "col"), P("col"), P("row", "col"), P("row", "col")),
        out_specs=(P("row", "col"), P("row", "col")),
        check_vma=False,
    )
```

```python
import jax
import jax.numpy as jnp
from jax import lax
from jax.experimental import pallas as pl
from jax.experimental.pallas import tpu as pltpu
from jax.sharding import PartitionSpec as P

X, Z_HI, Z_LO, Y = 4, 4, 2, 8
CHIPS = Z_LO * Y
PATCHES = 256
HALF = 512
TOK = 1024
K_DEV, K_CHIP, K_ALL = 24, 48, 768
FF_DEV = 768
BLOCKS = ((0, 256), (256, 256), (512, 128), (640, 128))
ORDER = (1, 0, 2, 3)
FB, NF = 256, len(BLOCKS)
X_ROWS, OUT_ROWS = K_ALL // X, K_ALL // (X * Z_HI)
TILE = 256


def kernel(
    partner, mix, act, weight_in, bias_in, earlier_in, cot_in,
    hidden, grad_out,
    ax, images, own, sel, cand_0, cand_1, ball, blend_t, weight, bias, earlier, cot, grad, zterm, zin, term, rx, zs, rz,
    send_a, recv_a, send_p, recv_p, send_y, recv_y, send_d, recv_d, send_l, recv_l, send_s, recv_s,
    send_rx, recv_rx, send_rz, recv_rz, local_a, local_in,
):
    row, col = lax.axis_index("row"), lax.axis_index("col")
    x, zh = lax.div(row, Z_HI), lax.rem(row, Z_HI)
    chip, core = lax.div(col, 2), lax.rem(col, 2)
    zl, y = lax.div(chip, Y), lax.rem(chip, Y)
    other_core = 1 - core
    f32, bf16 = jnp.float32, jnp.bfloat16

    def device(dx=0, dz=0, dl=0, dy=0, dh=0):
        r = lax.rem(x + dx, X) * Z_HI + lax.rem(zh + dz, Z_HI)
        c = (lax.rem(zl + dl, Z_LO) * Y + lax.rem(y + dy, Y)) * 2 + lax.rem(core + dh, 2)
        return {"row": r, "col": c}

    def remote(src, dst, send, recv, to):
        return pltpu.make_async_remote_copy(
            src_ref=src, dst_ref=dst, send_sem=send, recv_sem=recv,
            device_id=to, device_id_type=pl.DeviceIdType.MESH,
        )

    loads = [
        pltpu.make_async_copy(weight_in, weight, local_in.at[0]),
        pltpu.make_async_copy(bias_in, bias, local_in.at[3]),
        pltpu.make_async_copy(earlier_in, earlier, local_in.at[1]),
        pltpu.make_async_copy(cot_in, cot, local_in.at[2]),
    ]
    mine = [
        pltpu.make_async_copy(act, ax.at[x], local_a.at[0]),
        pltpu.make_async_copy(act.at[:, pl.ds(pl.multiple_of(core * HALF, HALF), HALF)], own.at[0], local_a.at[1]),
    ]
    for copy in mine:
        copy.start()

    barrier = pltpu.get_barrier_semaphore()
    peers = [device(dx=d) for d in range(1, X)]
    peers += [device(dz=d, dh=h) for d in range(Z_HI) for h in range(2) if d or h]
    peers += [device(dl=1)] + [device(dl=l, dy=d) for l in range(Z_LO) for d in (1, 2, Y - 2, Y - 1)]
    for peer in peers:
        pl.semaphore_signal(barrier, inc=1, device_id=peer, device_id_type=pl.DeviceIdType.MESH)
    pl.semaphore_wait(barrier, len(peers))

    cand = (cand_0, cand_1)

    first = [remote(act, ax.at[x], send_a.at[d], recv_a.at[d], device(dx=d)) for d in (2, 1, 3)]
    first.append(
        remote(
            act.at[:, pl.ds(pl.multiple_of(other_core * HALF, HALF), HALF)],
            own.at[1], send_a.at[0], recv_a.at[0], device(dh=1),
        )
    )
    for copy in first:
        copy.start()
    for copy in loads:
        copy.start()
    mine[0].wait()
    for copy in first[:3]:
        copy.wait_recv()
    for i in range(X):
        for j in range(4):
            images[i * 4 + j] = ax[i, :, j * PATCHES : (j + 1) * PATCHES]

    second = []
    for i in range(2):
        for d, h in ((2, 0), (2, 1), (1, 0), (1, 1), (3, 0), (3, 1), (0, 1), (0, 0)):
            to_row = x * Z_HI + lax.rem(zh + d, Z_HI)
            image = partner[to_row * 4 + lax.rem(core + h, 2) * 2 + i]
            value = images[lax.div(image, 16) * 4 + lax.rem(image, 4)]
            if d or h:
                sel[i, d, h] = value
                copy = remote(sel.at[i, d, h], cand[i].at[d, h], send_p.at[i, d, h], recv_p.at[i, d, h], device(dz=d, dh=h))
                copy.start()
                second.append(copy)
            else:
                cand[i][0, 0] = value
    mine[1].wait()
    first[3].wait_recv()

    def blend(i):
        for copy in second[7 * i : 7 * i + 7]:
            copy.wait_recv()
        image = row * 4 + core * 2 + i
        source = lax.rem(lax.div(partner[image], 4), Z_HI)
        slot = lax.rem(zh - source + Z_HI, Z_HI)
        share = mix[image].astype(f32) / 256.0
        span = slice(i * PATCHES, (i + 1) * PATCHES)
        parts = []
        for k in range(2):
            rel = lax.rem(core + k, 2)
            parts.append(share * own[rel, :, span].astype(f32) + (1.0 - share) * cand[i][slot, rel].astype(f32))
        ball[core, chip, :, span] = jnp.concatenate(parts, axis=0).astype(bf16)

    pending = []

    def start(copy):
        copy.start()
        pending.append(copy)
        return copy

    def place(plane, dy):
        return ball.at[core, lax.rem(zl + plane, Z_LO) * Y + lax.rem(y + dy, Y)]

    def image_of(off, i):
        return place(0, off).at[:, i * PATCHES : (i + 1) * PATCHES]

    def along_y(i, off, step, at):
        block = image_of(off, i)
        start(remote(block, block, send_y.at[i, at], recv_y.at[i, at], device(dy=step)))

    def aslant(i, off, step, at):
        block = image_of(off, i)
        start(remote(block, block, send_d.at[i, at], recv_d.at[i, at], device(dl=1, dy=step)))

    def to_sibling(plane, off):
        block = place(plane, off)
        start(remote(block, block, send_s.at[plane, off], recv_s.at[plane, off], device(dh=1)))

    def wait_for(block, sem):
        pltpu.make_async_copy(block, block, sem).wait()

    def onward(i):
        for off in (6, 2):
            wait_for(image_of(off, i), recv_y.at[i, off])
        off, step = 6 - 4 * core, 2 + 4 * core
        along_y(i, off, step, 4)
        aslant(i, off, step, 4)
        for off, step, at in ((6, 1, 5), (2, 7, 3)):
            along_y(i, off, step, at)
            aslant(i, off, step, at)

    def across(off):
        block = place(0, off)
        start(remote(block, block, send_l.at[off], recv_l.at[off], device(dl=1)))

    for i in range(2):
        blend(i)
        if i:
            across(0)
        for step in (2, 6, 1, 7):
            along_y(i, 0, step, Y - step)
    to_sibling(0, 0)
    block = place(1, 0)
    wait_for(block, recv_l.at[0])
    for step in (1, 7):
        start(remote(block, block, send_l.at[Y - step], recv_l.at[Y - step], device(dy=step)))
    to_sibling(1, 0)
    onward(0)
    for off in (7, 1):
        for i in range(2):
            wait_for(image_of(off, i), recv_y.at[i, off])
        to_sibling(0, off)
    onward(1)
    for off in (6, 2):
        across(off)
        to_sibling(0, off)
    for off in (7, 1, 6, 2):
        wait_for(place(1, off), recv_l.at[off])
        to_sibling(1, off)
    for off in (5, 3, 4):
        for i in range(2):
            wait_for(image_of(off, i), recv_y.at[i, off])
        to_sibling(0, off)
    for off in (5, 3, 4):
        for i in range(2):
            wait_for(place(1, off).at[:, i * PATCHES : (i + 1) * PATCHES], recv_d.at[i, off])
        to_sibling(1, off)
    for plane in range(Z_LO):
        for off in range(Y):
            block = ball.at[other_core, lax.rem(zl + plane, Z_LO) * Y + lax.rem(y + off, Y)]
            wait_for(block, recv_s.at[plane, off])

    def flip(t, carry):
        at = pl.ds(pl.multiple_of(t * 128, 128), 128)
        for h in range(2):
            rows = pl.ds(pl.multiple_of(h * HALF + t * 128, 128), 128)
            for b in range(Z_LO):
                block = ball[h, b * Y : (b + 1) * Y, :, at].reshape(Y * K_CHIP, 128)
                blend_t[rows, b * Y * K_CHIP : (b + 1) * Y * K_CHIP] = block.T
        return carry

    lax.fori_loop(0, HALF // 128, flip, 0)
    for copy in loads:
        copy.wait()

    def forward(f):
        at, width = BLOCKS[f]
        cols = slice(at, at + width)
        for t in range(TOK // TILE):
            rows = slice(t * TILE, (t + 1) * TILE)
            product = jnp.dot(blend_t[rows, :], weight[:, cols], preferred_element_type=f32)
            preact = earlier[rows, cols].astype(f32) + product + bias[cols]
            normal_cdf = 0.5 * (1.0 + lax.erf(preact * 0.7071067811865476))
            density = jnp.exp(-0.5 * preact * preact) * 0.3989422804014327
            hidden[rows, cols] = (preact * normal_cdf).astype(bf16)
            grad[rows, :width] = (cot[rows, cols].astype(f32) * (normal_cdf + preact * density)).astype(bf16)

    def terms(load, width):
        total = sum(
            jnp.dot(load(h), grad[h * HALF : (h + 1) * HALF, :width], preferred_element_type=f32) for h in range(2)
        )
        return total.astype(bf16)

    def over_x(f, d, src, dst):
        return start(remote(src, dst, send_rx.at[f, d - 1], recv_rx.at[f, d - 1], device(dx=d)))

    def over_z(f, d, src, dst):
        return start(remote(src, dst, send_rz.at[f, d - 1], recv_rz.at[f, d - 1], device(dz=d)))

    begun = {}
    for f, (at, width) in enumerate(BLOCKS):
        forward(f)
        cols = slice(at, at + width)
        begun[f] = []
        for d in (2, 1, 3, 0):
            if f == 0:
                to_z = lax.rem(zh + d, Z_HI)

                def load(h, to_z=to_z):
                    return jnp.concatenate([ball[h, Z_HI * k + to_z] for k in range(X)], axis=0)

                zterm[d] = terms(load, width).reshape(X, OUT_ROWS, width)
                if d:
                    begun[f].append(over_z(f, d, zterm.at[d], zin.at[d - 1]))
            else:
                to_x = lax.rem(x + d, X)

                def load(h, to_x=to_x):
                    return ball[h, pl.ds(to_x * Z_HI, Z_HI)].reshape(X_ROWS, HALF)

                term[d, :, cols] = terms(load, width)
                if d:
                    begun[f].append(over_x(f, d, term.at[d, :, cols], rx.at[d - 1, :, cols]))

    ends = {}
    for f in ORDER:
        at, width = BLOCKS[f]
        cols = slice(at, at + width)
        for copy in begun[f]:
            copy.wait_recv()
        for q in range(X):
            if f == 0:
                total = zterm[0, q].astype(f32)
                for d in range(1, Z_HI):
                    total = total + zin[d - 1, q].astype(f32)
            else:
                rows = slice(q * OUT_ROWS, (q + 1) * OUT_ROWS)
                total = term[0, rows, cols].astype(f32)
                for d in range(1, X):
                    total = total + rx[d - 1, rows, cols].astype(f32)
            zs[q, :, cols] = total.astype(bf16)
        ends[f] = []
        for d in (2, 1, 3):
            to = lax.rem(zh + d, Z_HI) if f else lax.rem(x + d, X)
            ends[f].append((over_z if f else over_x)(f, d, zs.at[to, :, cols], rz.at[d - 1, :, cols]))
    for f in ORDER:
        at, width = BLOCKS[f]
        cols = slice(at, at + width)
        for copy in ends[f]:
            copy.wait_recv()
        total = zs[zh if f else x, :, cols].astype(f32)
        for d in range(1, Z_HI):
            total = total + rz[d - 1, :, cols].astype(f32)
        grad_out[:, cols] = total

    for copy in first + second + pending:
        copy.wait_send()


def write_out(hidden, grad, hidden_out, grad_out, sems):
    copies = [
        pltpu.make_async_copy(hidden, hidden_out, sems.at[0]),
        pltpu.make_async_copy(grad, grad_out, sems.at[1]),
    ]
    for copy in copies:
        copy.start()
    for copy in copies:
        copy.wait()


def local(activations, partner, mix_weight, weight, bias, earlier, cotangent):
    bf16, dma = jnp.bfloat16, pltpu.SemaphoreType.DMA
    hbm, vmem, smem = (pl.BlockSpec(memory_space=s) for s in (pl.ANY, pltpu.VMEM, pltpu.SMEM))
    hidden, grad = pl.pallas_call(
        kernel,
        out_shape=(
            pltpu.VMEM((TOK, FF_DEV), bf16),
            pltpu.VMEM((OUT_ROWS, FF_DEV), jnp.float32),
        ),
        in_specs=[smem, smem, hbm, hbm, hbm, hbm, hbm],
        out_specs=(vmem, vmem),
        scratch_shapes=[
            pltpu.VMEM((X, K_DEV, TOK), bf16),
            pltpu.VMEM((X * 4, K_DEV, PATCHES), bf16),
            pltpu.VMEM((2, K_DEV, HALF), bf16),
            pltpu.VMEM((2, Z_HI, 2, K_DEV, PATCHES), bf16),
            pltpu.VMEM((Z_HI, 2, K_DEV, PATCHES), bf16),
            pltpu.VMEM((Z_HI, 2, K_DEV, PATCHES), bf16),
            pltpu.VMEM((2, CHIPS, K_CHIP, HALF), bf16),
            pltpu.VMEM((TOK, K_ALL), bf16),
            pltpu.VMEM((K_ALL, FF_DEV), bf16),
            pltpu.VMEM((FF_DEV,), jnp.float32),
            pltpu.VMEM((TOK, FF_DEV), bf16),
            pltpu.VMEM((TOK, FF_DEV), bf16),
            pltpu.VMEM((TOK, FB), bf16),
            pltpu.VMEM((Z_HI, X, OUT_ROWS, FB), bf16),
            pltpu.VMEM((Z_HI - 1, X, OUT_ROWS, FB), bf16),
            pltpu.VMEM((X, X_ROWS, FF_DEV), bf16),
            pltpu.VMEM((X - 1, X_ROWS, FF_DEV), bf16),
            pltpu.VMEM((Z_HI, OUT_ROWS, FF_DEV), bf16),
            pltpu.VMEM((Z_HI - 1, OUT_ROWS, FF_DEV), bf16),
            dma((X,)), dma((X,)),
            dma((2, Z_HI, 2)), dma((2, Z_HI, 2)),
            dma((2, Y)), dma((2, Y)), dma((2, Y)), dma((2, Y)), dma((Y,)), dma((Y,)),
            dma((2, Y)), dma((2, Y)),
            dma((NF, X - 1)), dma((NF, X - 1)),
            dma((NF, Z_HI - 1)), dma((NF, Z_HI - 1)),
            dma((2,)), dma((4,)),
        ],
        compiler_params=pltpu.CompilerParams(
            collective_id=0, has_side_effects=True, vmem_limit_bytes=56 * 2**20
        ),
    )(partner, mix_weight, activations.T, weight, bias, earlier, cotangent)
    hidden, grad = (pltpu.with_memory_space_constraint(a, pltpu.VMEM) for a in (hidden, grad))
    return pl.pallas_call(
        write_out,
        out_shape=(
            jax.ShapeDtypeStruct((TOK, FF_DEV), bf16),
            jax.ShapeDtypeStruct((OUT_ROWS, FF_DEV), jnp.float32),
        ),
        in_specs=[hbm, hbm],
        out_specs=(hbm, hbm),
        scratch_shapes=[dma((2,))],
    )(hidden, grad)


def solution(mesh):
    return jax.shard_map(
        local,
        mesh=mesh,
        in_specs=(P("row", "col"), P(), P(), P(None, "col"), P("col"), P("row", "col"), P("row", "col")),
        out_specs=(P("row", "col"), P("row", "col")),
        check_vma=False,
    )
```

```python
import jax
import jax.numpy as jnp
from jax import lax
from jax.experimental import pallas as pl
from jax.experimental.pallas import tpu as pltpu
from jax.sharding import PartitionSpec as P

X, Z_HI, Z_LO, Y = 4, 4, 2, 8
CHIPS = Z_LO * Y
PATCHES = 256
HALF = 512
TOK = 1024
K_DEV, K_CHIP, K_ALL = 24, 48, 768
FF_DEV = 768
BLOCKS = ((0, 256), (256, 256), (512, 128), (640, 128))
ORDER = (1, 0, 2, 3)
GROUPS = ((0, 1), (2,), (3,))
FB, NF = 256, len(BLOCKS)
X_ROWS, OUT_ROWS = K_ALL // X, K_ALL // (X * Z_HI)
TILE = 256


def kernel(
    partner, mix, act, weight_in, bias_in, earlier_in, cot_in,
    hidden, grad_out,
    ax, images, own, sel, cand_0, cand_1, ball, blend_t, weight, bias, earlier, cot, grad, zterm, zin, term, rx, zs, rz,
    send_a, recv_a, send_p, recv_p, send_y, recv_y, send_d, recv_d, send_l, recv_l, send_s, recv_s,
    send_rx, recv_rx, send_rz, recv_rz, local_a, local_in,
):
    row, col = lax.axis_index("row"), lax.axis_index("col")
    x, zh = lax.div(row, Z_HI), lax.rem(row, Z_HI)
    chip, core = lax.div(col, 2), lax.rem(col, 2)
    zl, y = lax.div(chip, Y), lax.rem(chip, Y)
    other_core = 1 - core
    f32, bf16 = jnp.float32, jnp.bfloat16

    def device(dx=0, dz=0, dl=0, dy=0, dh=0):
        r = lax.rem(x + dx, X) * Z_HI + lax.rem(zh + dz, Z_HI)
        c = (lax.rem(zl + dl, Z_LO) * Y + lax.rem(y + dy, Y)) * 2 + lax.rem(core + dh, 2)
        return {"row": r, "col": c}

    def remote(src, dst, send, recv, to):
        return pltpu.make_async_remote_copy(
            src_ref=src, dst_ref=dst, send_sem=send, recv_sem=recv,
            device_id=to, device_id_type=pl.DeviceIdType.MESH,
        )

    loads = [
        pltpu.make_async_copy(weight_in, weight, local_in.at[0]),
        pltpu.make_async_copy(bias_in, bias, local_in.at[3]),
        pltpu.make_async_copy(earlier_in, earlier, local_in.at[1]),
        pltpu.make_async_copy(cot_in, cot, local_in.at[2]),
    ]
    mine = [
        pltpu.make_async_copy(act, ax.at[x], local_a.at[0]),
        pltpu.make_async_copy(act.at[:, pl.ds(pl.multiple_of(core * HALF, HALF), HALF)], own.at[0], local_a.at[1]),
    ]
    for copy in mine:
        copy.start()

    barrier = pltpu.get_barrier_semaphore()
    peers = [device(dx=d) for d in range(1, X)]
    peers += [device(dz=d, dh=h) for d in range(Z_HI) for h in range(2) if d or h]
    peers += [device(dl=1)] + [device(dl=l, dy=d) for l in range(Z_LO) for d in (1, 2, Y - 2, Y - 1)]
    for peer in peers:
        pl.semaphore_signal(barrier, inc=1, device_id=peer, device_id_type=pl.DeviceIdType.MESH)
    pl.semaphore_wait(barrier, len(peers))

    cand = (cand_0, cand_1)

    first = [remote(act, ax.at[x], send_a.at[d], recv_a.at[d], device(dx=d)) for d in (2, 1, 3)]
    first.append(
        remote(
            act.at[:, pl.ds(pl.multiple_of(other_core * HALF, HALF), HALF)],
            own.at[1], send_a.at[0], recv_a.at[0], device(dh=1),
        )
    )
    for copy in first:
        copy.start()
    for copy in loads:
        copy.start()
    mine[0].wait()
    for copy in first[:3]:
        copy.wait_recv()
    for i in range(X):
        for j in range(4):
            images[i * 4 + j] = ax[i, :, j * PATCHES : (j + 1) * PATCHES]

    second = []
    for i in range(2):
        for d, h in ((2, 0), (2, 1), (1, 0), (1, 1), (3, 0), (3, 1), (0, 1), (0, 0)):
            to_row = x * Z_HI + lax.rem(zh + d, Z_HI)
            image = partner[to_row * 4 + lax.rem(core + h, 2) * 2 + i]
            value = images[lax.div(image, 16) * 4 + lax.rem(image, 4)]
            if d or h:
                sel[i, d, h] = value
                copy = remote(sel.at[i, d, h], cand[i].at[d, h], send_p.at[i, d, h], recv_p.at[i, d, h], device(dz=d, dh=h))
                copy.start()
                second.append(copy)
            else:
                cand[i][0, 0] = value
    mine[1].wait()
    first[3].wait_recv()

    def blend(i):
        for copy in second[7 * i : 7 * i + 7]:
            copy.wait_recv()
        image = row * 4 + core * 2 + i
        source = lax.rem(lax.div(partner[image], 4), Z_HI)
        slot = lax.rem(zh - source + Z_HI, Z_HI)
        share = mix[image].astype(f32) / 256.0
        span = slice(i * PATCHES, (i + 1) * PATCHES)
        parts = []
        for k in range(2):
            rel = lax.rem(core + k, 2)
            parts.append(share * own[rel, :, span].astype(f32) + (1.0 - share) * cand[i][slot, rel].astype(f32))
        ball[core, chip, :, span] = jnp.concatenate(parts, axis=0).astype(bf16)

    pending = []

    def start(copy):
        copy.start()
        pending.append(copy)
        return copy

    def place(plane, dy):
        return ball.at[core, lax.rem(zl + plane, Z_LO) * Y + lax.rem(y + dy, Y)]

    def image_of(off, i):
        return place(0, off).at[:, i * PATCHES : (i + 1) * PATCHES]

    def along_y(i, off, step, at):
        block = image_of(off, i)
        start(remote(block, block, send_y.at[i, at], recv_y.at[i, at], device(dy=step)))

    def aslant(i, off, step, at):
        block = image_of(off, i)
        start(remote(block, block, send_d.at[i, at], recv_d.at[i, at], device(dl=1, dy=step)))

    def to_sibling(plane, off):
        block = place(plane, off)
        start(remote(block, block, send_s.at[plane, off], recv_s.at[plane, off], device(dh=1)))

    def wait_for(block, sem):
        pltpu.make_async_copy(block, block, sem).wait()

    def onward(i):
        for off in (6, 2):
            wait_for(image_of(off, i), recv_y.at[i, off])
        off, step = 6 - 4 * core, 2 + 4 * core
        along_y(i, off, step, 4)
        aslant(i, off, step, 4)
        for off, step, at in ((6, 1, 5), (2, 7, 3)):
            along_y(i, off, step, at)
            aslant(i, off, step, at)

    def across(off):
        block = place(0, off)
        start(remote(block, block, send_l.at[off], recv_l.at[off], device(dl=1)))

    for i in range(2):
        blend(i)
        if i:
            across(0)
        for step in (2, 6, 1, 7):
            along_y(i, 0, step, Y - step)
    to_sibling(0, 0)
    block = place(1, 0)
    wait_for(block, recv_l.at[0])
    for step in (1, 7):
        start(remote(block, block, send_l.at[Y - step], recv_l.at[Y - step], device(dy=step)))
    to_sibling(1, 0)
    onward(0)
    for off in (7, 1):
        for i in range(2):
            wait_for(image_of(off, i), recv_y.at[i, off])
        to_sibling(0, off)
    onward(1)
    for off in (6, 2):
        across(off)
        to_sibling(0, off)
    for off in (7, 1, 6, 2):
        wait_for(place(1, off), recv_l.at[off])
        to_sibling(1, off)
    for off in (5, 3, 4):
        for i in range(2):
            wait_for(image_of(off, i), recv_y.at[i, off])
        to_sibling(0, off)
    for off in (5, 3, 4):
        for i in range(2):
            wait_for(place(1, off).at[:, i * PATCHES : (i + 1) * PATCHES], recv_d.at[i, off])
        to_sibling(1, off)
    def flip(h):
        for t in range(HALF // 128):
            at = slice(t * 128, (t + 1) * 128)
            rows = pl.ds(pl.multiple_of(h * HALF + t * 128, 128), 128)
            for b in range(Z_LO):
                block = ball[h, b * Y : (b + 1) * Y, :, at].reshape(Y * K_CHIP, 128)
                blend_t[rows, b * Y * K_CHIP : (b + 1) * Y * K_CHIP] = block.T

    def forward(f, h):
        at, width = BLOCKS[f]
        cols = slice(at, at + width)
        for t in range(HALF // TILE):
            rows = pl.ds(pl.multiple_of(h * HALF + t * TILE, TILE), TILE)
            product = jnp.dot(blend_t[rows, :], weight[:, cols], preferred_element_type=f32)
            preact = earlier[rows, cols].astype(f32) + product + bias[cols]
            normal_cdf = 0.5 * (1.0 + lax.erf(preact * 0.7071067811865476))
            density = jnp.exp(-0.5 * preact * preact) * 0.3989422804014327
            hidden[rows, cols] = (preact * normal_cdf).astype(bf16)
            grad[rows, cols] = (cot[rows, cols].astype(f32) * (normal_cdf + preact * density)).astype(bf16)

    for copy in loads:
        copy.wait()
    flip(core)
    for f in range(NF):
        forward(f, core)
    for plane in range(Z_LO):
        for off in range(Y):
            block = ball.at[other_core, lax.rem(zl + plane, Z_LO) * Y + lax.rem(y + off, Y)]
            wait_for(block, recv_s.at[plane, off])
    flip(other_core)

    def terms(load, cols):
        total = sum(
            jnp.dot(load(h), grad[h * HALF : (h + 1) * HALF, cols], preferred_element_type=f32) for h in range(2)
        )
        return total.astype(bf16)

    def over_x(f, d, src, dst):
        return start(remote(src, dst, send_rx.at[f, d - 1], recv_rx.at[f, d - 1], device(dx=d)))

    def over_z(f, d, src, dst):
        return start(remote(src, dst, send_rz.at[f, d - 1], recv_rz.at[f, d - 1], device(dz=d)))

    begun = {f: [] for f in range(NF)}

    def first_sum(f, d):
        at, width = BLOCKS[f]
        cols = slice(at, at + width)
        if f == 0:
            to_z = lax.rem(zh + d, Z_HI)
            total = terms(lambda h: jnp.concatenate([ball[h, Z_HI * k + to_z] for k in range(X)], axis=0), cols)
            zterm[d] = total.reshape(X, OUT_ROWS, width)
            if d:
                begun[f].append(over_z(f, d, zterm.at[d], zin.at[d - 1]))
        else:
            to_x = lax.rem(x + d, X)
            term[d, :, cols] = terms(lambda h: ball[h, pl.ds(to_x * Z_HI, Z_HI)].reshape(X_ROWS, HALF), cols)
            if d:
                begun[f].append(over_x(f, d, term.at[d, :, cols], rx.at[d - 1, :, cols]))

    for group in GROUPS:
        for f in group:
            forward(f, other_core)
        for d in (2, 1, 3, 0):
            for f in group:
                first_sum(f, d)

    ends = {}
    for f in ORDER:
        at, width = BLOCKS[f]
        cols = slice(at, at + width)
        for copy in begun[f]:
            copy.wait_recv()
        for q in range(X):
            if f == 0:
                total = zterm[0, q].astype(f32)
                for d in range(1, Z_HI):
                    total = total + zin[d - 1, q].astype(f32)
            else:
                rows = slice(q * OUT_ROWS, (q + 1) * OUT_ROWS)
                total = term[0, rows, cols].astype(f32)
                for d in range(1, X):
                    total = total + rx[d - 1, rows, cols].astype(f32)
            zs[q, :, cols] = total.astype(bf16)
        ends[f] = []
        for d in (2, 1, 3):
            to = lax.rem(zh + d, Z_HI) if f else lax.rem(x + d, X)
            ends[f].append((over_z if f else over_x)(f, d, zs.at[to, :, cols], rz.at[d - 1, :, cols]))
    for f in ORDER:
        at, width = BLOCKS[f]
        cols = slice(at, at + width)
        for copy in ends[f]:
            copy.wait_recv()
        total = zs[zh if f else x, :, cols].astype(f32)
        for d in range(1, Z_HI):
            total = total + rz[d - 1, :, cols].astype(f32)
        grad_out[:, cols] = total

    for copy in first + second + pending:
        copy.wait_send()


def write_out(hidden, grad, hidden_out, grad_out, sems):
    copies = [
        pltpu.make_async_copy(hidden, hidden_out, sems.at[0]),
        pltpu.make_async_copy(grad, grad_out, sems.at[1]),
    ]
    for copy in copies:
        copy.start()
    for copy in copies:
        copy.wait()


def local(activations, partner, mix_weight, weight, bias, earlier, cotangent):
    bf16, dma = jnp.bfloat16, pltpu.SemaphoreType.DMA
    hbm, vmem, smem = (pl.BlockSpec(memory_space=s) for s in (pl.ANY, pltpu.VMEM, pltpu.SMEM))
    hidden, grad = pl.pallas_call(
        kernel,
        out_shape=(
            pltpu.VMEM((TOK, FF_DEV), bf16),
            pltpu.VMEM((OUT_ROWS, FF_DEV), jnp.float32),
        ),
        in_specs=[smem, smem, hbm, hbm, hbm, hbm, hbm],
        out_specs=(vmem, vmem),
        scratch_shapes=[
            pltpu.VMEM((X, K_DEV, TOK), bf16),
            pltpu.VMEM((X * 4, K_DEV, PATCHES), bf16),
            pltpu.VMEM((2, K_DEV, HALF), bf16),
            pltpu.VMEM((2, Z_HI, 2, K_DEV, PATCHES), bf16),
            pltpu.VMEM((Z_HI, 2, K_DEV, PATCHES), bf16),
            pltpu.VMEM((Z_HI, 2, K_DEV, PATCHES), bf16),
            pltpu.VMEM((2, CHIPS, K_CHIP, HALF), bf16),
            pltpu.VMEM((TOK, K_ALL), bf16),
            pltpu.VMEM((K_ALL, FF_DEV), bf16),
            pltpu.VMEM((FF_DEV,), jnp.float32),
            pltpu.VMEM((TOK, FF_DEV), bf16),
            pltpu.VMEM((TOK, FF_DEV), bf16),
            pltpu.VMEM((TOK, FF_DEV), bf16),
            pltpu.VMEM((Z_HI, X, OUT_ROWS, FB), bf16),
            pltpu.VMEM((Z_HI - 1, X, OUT_ROWS, FB), bf16),
            pltpu.VMEM((X, X_ROWS, FF_DEV), bf16),
            pltpu.VMEM((X - 1, X_ROWS, FF_DEV), bf16),
            pltpu.VMEM((Z_HI, OUT_ROWS, FF_DEV), bf16),
            pltpu.VMEM((Z_HI - 1, OUT_ROWS, FF_DEV), bf16),
            dma((X,)), dma((X,)),
            dma((2, Z_HI, 2)), dma((2, Z_HI, 2)),
            dma((2, Y)), dma((2, Y)), dma((2, Y)), dma((2, Y)), dma((Y,)), dma((Y,)),
            dma((2, Y)), dma((2, Y)),
            dma((NF, X - 1)), dma((NF, X - 1)),
            dma((NF, Z_HI - 1)), dma((NF, Z_HI - 1)),
            dma((2,)), dma((4,)),
        ],
        compiler_params=pltpu.CompilerParams(
            collective_id=0, has_side_effects=True, vmem_limit_bytes=56 * 2**20
        ),
    )(partner, mix_weight, activations.T, weight, bias, earlier, cotangent)
    hidden, grad = (pltpu.with_memory_space_constraint(a, pltpu.VMEM) for a in (hidden, grad))
    return pl.pallas_call(
        write_out,
        out_shape=(
            jax.ShapeDtypeStruct((TOK, FF_DEV), bf16),
            jax.ShapeDtypeStruct((OUT_ROWS, FF_DEV), jnp.float32),
        ),
        in_specs=[hbm, hbm],
        out_specs=(hbm, hbm),
        scratch_shapes=[dma((2,))],
    )(hidden, grad)


def solution(mesh):
    return jax.shard_map(
        local,
        mesh=mesh,
        in_specs=(P("row", "col"), P(), P(), P(None, "col"), P("col"), P("row", "col"), P("row", "col")),
        out_specs=(P("row", "col"), P("row", "col")),
        check_vma=False,
    )
```

```python
import jax
import jax.numpy as jnp
from jax import lax
from jax.experimental import pallas as pl
from jax.experimental.pallas import tpu as pltpu
from jax.sharding import PartitionSpec as P

X, Z_HI, Z_LO, Y = 4, 4, 2, 8
CHIPS = Z_LO * Y
PATCHES = 256
HALF = 512
TOK = 1024
K_DEV, K_CHIP, K_ALL = 24, 48, 768
FF_DEV = 768
BLOCKS = ((0, 256), (256, 256), (512, 128), (640, 128))
ORDER = (1, 2, 3, 0)
GROUPS = ((0,), (1,), (2,), (3,))
FB, NF = 256, len(BLOCKS)
X_ROWS, OUT_ROWS = K_ALL // X, K_ALL // (X * Z_HI)
TILE = 256


def kernel(
    partner, mix, act, weight_in, bias_in, earlier_in, cot_in,
    hidden, grad_out,
    ax, images, own, sel, cand_0, cand_1, ball, blend_t, weight, bias, earlier, cot, grad, zterm, zin, term, rx, zs, rz,
    send_a, recv_a, send_p, recv_p, send_y, recv_y, send_d, recv_d, send_l, recv_l, send_s, recv_s,
    send_rx, recv_rx, send_rz, recv_rz, local_a, local_in,
):
    row, col = lax.axis_index("row"), lax.axis_index("col")
    x, zh = lax.div(row, Z_HI), lax.rem(row, Z_HI)
    chip, core = lax.div(col, 2), lax.rem(col, 2)
    zl, y = lax.div(chip, Y), lax.rem(chip, Y)
    other_core = 1 - core
    f32, bf16 = jnp.float32, jnp.bfloat16

    def device(dx=0, dz=0, dl=0, dy=0, dh=0):
        r = lax.rem(x + dx, X) * Z_HI + lax.rem(zh + dz, Z_HI)
        c = (lax.rem(zl + dl, Z_LO) * Y + lax.rem(y + dy, Y)) * 2 + lax.rem(core + dh, 2)
        return {"row": r, "col": c}

    def remote(src, dst, send, recv, to):
        return pltpu.make_async_remote_copy(
            src_ref=src, dst_ref=dst, send_sem=send, recv_sem=recv,
            device_id=to, device_id_type=pl.DeviceIdType.MESH,
        )

    loads = [
        pltpu.make_async_copy(weight_in, weight, local_in.at[0]),
        pltpu.make_async_copy(bias_in, bias, local_in.at[3]),
        pltpu.make_async_copy(earlier_in, earlier, local_in.at[1]),
        pltpu.make_async_copy(cot_in, cot, local_in.at[2]),
    ]
    mine = [
        pltpu.make_async_copy(act, ax.at[x], local_a.at[0]),
        pltpu.make_async_copy(act.at[:, pl.ds(pl.multiple_of(core * HALF, HALF), HALF)], own.at[0], local_a.at[1]),
    ]
    for copy in mine:
        copy.start()

    barrier = pltpu.get_barrier_semaphore()
    peers = [device(dx=d) for d in range(1, X)]
    peers += [device(dz=d, dh=h) for d in range(Z_HI) for h in range(2) if d or h]
    peers += [device(dl=1)] + [device(dl=l, dy=d) for l in range(Z_LO) for d in (1, 2, Y - 2, Y - 1)]
    for peer in peers:
        pl.semaphore_signal(barrier, inc=1, device_id=peer, device_id_type=pl.DeviceIdType.MESH)
    pl.semaphore_wait(barrier, len(peers))

    cand = (cand_0, cand_1)

    first = [remote(act, ax.at[x], send_a.at[d], recv_a.at[d], device(dx=d)) for d in (2, 1, 3)]
    first.append(
        remote(
            act.at[:, pl.ds(pl.multiple_of(other_core * HALF, HALF), HALF)],
            own.at[1], send_a.at[0], recv_a.at[0], device(dh=1),
        )
    )
    for copy in first:
        copy.start()
    for copy in loads:
        copy.start()
    mine[0].wait()
    for copy in first[:3]:
        copy.wait_recv()
    for i in range(X):
        for j in range(4):
            images[i * 4 + j] = ax[i, :, j * PATCHES : (j + 1) * PATCHES]

    second = []
    for i in range(2):
        for d, h in ((2, 0), (2, 1), (1, 0), (1, 1), (3, 0), (3, 1), (0, 1), (0, 0)):
            to_row = x * Z_HI + lax.rem(zh + d, Z_HI)
            image = partner[to_row * 4 + lax.rem(core + h, 2) * 2 + i]
            value = images[lax.div(image, 16) * 4 + lax.rem(image, 4)]
            if d or h:
                sel[i, d, h] = value
                copy = remote(sel.at[i, d, h], cand[i].at[d, h], send_p.at[i, d, h], recv_p.at[i, d, h], device(dz=d, dh=h))
                copy.start()
                second.append(copy)
            else:
                cand[i][0, 0] = value
    mine[1].wait()
    first[3].wait_recv()

    def blend(i):
        for copy in second[7 * i : 7 * i + 7]:
            copy.wait_recv()
        image = row * 4 + core * 2 + i
        source = lax.rem(lax.div(partner[image], 4), Z_HI)
        slot = lax.rem(zh - source + Z_HI, Z_HI)
        share = mix[image].astype(f32) / 256.0
        span = slice(i * PATCHES, (i + 1) * PATCHES)
        parts = []
        for k in range(2):
            rel = lax.rem(core + k, 2)
            parts.append(share * own[rel, :, span].astype(f32) + (1.0 - share) * cand[i][slot, rel].astype(f32))
        ball[core, chip, :, span] = jnp.concatenate(parts, axis=0).astype(bf16)

    pending = []

    def start(copy):
        copy.start()
        pending.append(copy)
        return copy

    def place(plane, dy):
        return ball.at[core, lax.rem(zl + plane, Z_LO) * Y + lax.rem(y + dy, Y)]

    def image_of(off, i):
        return place(0, off).at[:, i * PATCHES : (i + 1) * PATCHES]

    def along_y(i, off, step, at):
        block = image_of(off, i)
        start(remote(block, block, send_y.at[i, at], recv_y.at[i, at], device(dy=step)))

    def aslant(i, off, step, at):
        block = image_of(off, i)
        start(remote(block, block, send_d.at[i, at], recv_d.at[i, at], device(dl=1, dy=step)))

    def to_sibling(plane, off):
        block = place(plane, off)
        start(remote(block, block, send_s.at[plane, off], recv_s.at[plane, off], device(dh=1)))

    def wait_for(block, sem):
        pltpu.make_async_copy(block, block, sem).wait()

    def onward(i):
        for off in (6, 2):
            wait_for(image_of(off, i), recv_y.at[i, off])
        off, step = 6 - 4 * core, 2 + 4 * core
        along_y(i, off, step, 4)
        aslant(i, off, step, 4)
        for off, step, at in ((6, 1, 5), (2, 7, 3)):
            along_y(i, off, step, at)
            aslant(i, off, step, at)

    def across(off):
        block = place(0, off)
        start(remote(block, block, send_l.at[off], recv_l.at[off], device(dl=1)))

    for i in range(2):
        blend(i)
        if i:
            across(0)
        for step in (2, 6, 1, 7):
            along_y(i, 0, step, Y - step)
    to_sibling(0, 0)
    block = place(1, 0)
    wait_for(block, recv_l.at[0])
    for step in (1, 7):
        start(remote(block, block, send_l.at[Y - step], recv_l.at[Y - step], device(dy=step)))
    to_sibling(1, 0)
    onward(0)
    for off in (7, 1):
        for i in range(2):
            wait_for(image_of(off, i), recv_y.at[i, off])
        to_sibling(0, off)
    onward(1)
    for off in (6, 2):
        across(off)
        to_sibling(0, off)
    for off in (7, 1, 6, 2):
        wait_for(place(1, off), recv_l.at[off])
        to_sibling(1, off)
    for off in (5, 3, 4):
        for i in range(2):
            wait_for(image_of(off, i), recv_y.at[i, off])
        to_sibling(0, off)
    for off in (5, 3, 4):
        for i in range(2):
            wait_for(place(1, off).at[:, i * PATCHES : (i + 1) * PATCHES], recv_d.at[i, off])
        to_sibling(1, off)
    def flip(h):
        for t in range(HALF // 128):
            at = slice(t * 128, (t + 1) * 128)
            rows = pl.ds(pl.multiple_of(h * HALF + t * 128, 128), 128)
            for b in range(Z_LO):
                block = ball[h, b * Y : (b + 1) * Y, :, at].reshape(Y * K_CHIP, 128)
                blend_t[rows, b * Y * K_CHIP : (b + 1) * Y * K_CHIP] = block.T

    def forward(f, h):
        at, width = BLOCKS[f]
        cols = slice(at, at + width)
        for t in range(HALF // TILE):
            rows = pl.ds(pl.multiple_of(h * HALF + t * TILE, TILE), TILE)
            product = jnp.dot(blend_t[rows, :], weight[:, cols], preferred_element_type=f32)
            preact = earlier[rows, cols].astype(f32) + product + bias[cols]
            normal_cdf = 0.5 * (1.0 + lax.erf(preact * 0.7071067811865476))
            density = jnp.exp(-0.5 * preact * preact) * 0.3989422804014327
            hidden[rows, cols] = (preact * normal_cdf).astype(bf16)
            grad[rows, cols] = (cot[rows, cols].astype(f32) * (normal_cdf + preact * density)).astype(bf16)

    for copy in loads:
        copy.wait()
    flip(core)
    for f in range(NF):
        forward(f, core)
    for plane in range(Z_LO):
        for off in range(Y):
            block = ball.at[other_core, lax.rem(zl + plane, Z_LO) * Y + lax.rem(y + off, Y)]
            wait_for(block, recv_s.at[plane, off])
    flip(other_core)

    def terms(load, cols):
        total = sum(
            jnp.dot(load(h), grad[h * HALF : (h + 1) * HALF, cols], preferred_element_type=f32) for h in range(2)
        )
        return total.astype(bf16)

    def over_x(f, d, src, dst):
        return start(remote(src, dst, send_rx.at[f, d - 1], recv_rx.at[f, d - 1], device(dx=d)))

    def over_z(f, d, src, dst):
        return start(remote(src, dst, send_rz.at[f, d - 1], recv_rz.at[f, d - 1], device(dz=d)))

    begun = {f: [] for f in range(NF)}

    def first_sum(f, d):
        at, width = BLOCKS[f]
        cols = slice(at, at + width)
        if f == 0:
            to_z = lax.rem(zh + d, Z_HI)
            total = terms(lambda h: jnp.concatenate([ball[h, Z_HI * k + to_z] for k in range(X)], axis=0), cols)
            zterm[d] = total.reshape(X, OUT_ROWS, width)
            if d:
                begun[f].append(over_z(f, d, zterm.at[d], zin.at[d - 1]))
        else:
            to_x = lax.rem(x + d, X)
            term[d, :, cols] = terms(lambda h: ball[h, pl.ds(to_x * Z_HI, Z_HI)].reshape(X_ROWS, HALF), cols)
            if d:
                begun[f].append(over_x(f, d, term.at[d, :, cols], rx.at[d - 1, :, cols]))

    for group in GROUPS:
        for f in group:
            forward(f, other_core)
        for d in (2, 1, 3, 0):
            for f in group:
                first_sum(f, d)

    ends = {}
    for f in ORDER:
        at, width = BLOCKS[f]
        cols = slice(at, at + width)
        for copy in begun[f]:
            copy.wait_recv()
        for q in range(X):
            if f == 0:
                total = zterm[0, q].astype(f32)
                for d in range(1, Z_HI):
                    total = total + zin[d - 1, q].astype(f32)
            else:
                rows = slice(q * OUT_ROWS, (q + 1) * OUT_ROWS)
                total = term[0, rows, cols].astype(f32)
                for d in range(1, X):
                    total = total + rx[d - 1, rows, cols].astype(f32)
            zs[q, :, cols] = total.astype(bf16)
        ends[f] = []
        for d in (2, 1, 3):
            to = lax.rem(zh + d, Z_HI) if f else lax.rem(x + d, X)
            ends[f].append((over_z if f else over_x)(f, d, zs.at[to, :, cols], rz.at[d - 1, :, cols]))
    for f in ORDER:
        at, width = BLOCKS[f]
        cols = slice(at, at + width)
        for copy in ends[f]:
            copy.wait_recv()
        total = zs[zh if f else x, :, cols].astype(f32)
        for d in range(1, Z_HI):
            total = total + rz[d - 1, :, cols].astype(f32)
        grad_out[:, cols] = total

    for copy in first + second + pending:
        copy.wait_send()


def write_out(hidden, grad, hidden_out, grad_out, sems):
    copies = [
        pltpu.make_async_copy(hidden, hidden_out, sems.at[0]),
        pltpu.make_async_copy(grad, grad_out, sems.at[1]),
    ]
    for copy in copies:
        copy.start()
    for copy in copies:
        copy.wait()


def local(activations, partner, mix_weight, weight, bias, earlier, cotangent):
    bf16, dma = jnp.bfloat16, pltpu.SemaphoreType.DMA
    hbm, vmem, smem = (pl.BlockSpec(memory_space=s) for s in (pl.ANY, pltpu.VMEM, pltpu.SMEM))
    hidden, grad = pl.pallas_call(
        kernel,
        out_shape=(
            pltpu.VMEM((TOK, FF_DEV), bf16),
            pltpu.VMEM((OUT_ROWS, FF_DEV), jnp.float32),
        ),
        in_specs=[smem, smem, hbm, hbm, hbm, hbm, hbm],
        out_specs=(vmem, vmem),
        scratch_shapes=[
            pltpu.VMEM((X, K_DEV, TOK), bf16),
            pltpu.VMEM((X * 4, K_DEV, PATCHES), bf16),
            pltpu.VMEM((2, K_DEV, HALF), bf16),
            pltpu.VMEM((2, Z_HI, 2, K_DEV, PATCHES), bf16),
            pltpu.VMEM((Z_HI, 2, K_DEV, PATCHES), bf16),
            pltpu.VMEM((Z_HI, 2, K_DEV, PATCHES), bf16),
            pltpu.VMEM((2, CHIPS, K_CHIP, HALF), bf16),
            pltpu.VMEM((TOK, K_ALL), bf16),
            pltpu.VMEM((K_ALL, FF_DEV), bf16),
            pltpu.VMEM((FF_DEV,), jnp.float32),
            pltpu.VMEM((TOK, FF_DEV), bf16),
            pltpu.VMEM((TOK, FF_DEV), bf16),
            pltpu.VMEM((TOK, FF_DEV), bf16),
            pltpu.VMEM((Z_HI, X, OUT_ROWS, FB), bf16),
            pltpu.VMEM((Z_HI - 1, X, OUT_ROWS, FB), bf16),
            pltpu.VMEM((X, X_ROWS, FF_DEV), bf16),
            pltpu.VMEM((X - 1, X_ROWS, FF_DEV), bf16),
            pltpu.VMEM((Z_HI, OUT_ROWS, FF_DEV), bf16),
            pltpu.VMEM((Z_HI - 1, OUT_ROWS, FF_DEV), bf16),
            dma((X,)), dma((X,)),
            dma((2, Z_HI, 2)), dma((2, Z_HI, 2)),
            dma((2, Y)), dma((2, Y)), dma((2, Y)), dma((2, Y)), dma((Y,)), dma((Y,)),
            dma((2, Y)), dma((2, Y)),
            dma((NF, X - 1)), dma((NF, X - 1)),
            dma((NF, Z_HI - 1)), dma((NF, Z_HI - 1)),
            dma((2,)), dma((4,)),
        ],
        compiler_params=pltpu.CompilerParams(
            collective_id=0, has_side_effects=True, vmem_limit_bytes=56 * 2**20
        ),
    )(partner, mix_weight, activations.T, weight, bias, earlier, cotangent)
    hidden, grad = (pltpu.with_memory_space_constraint(a, pltpu.VMEM) for a in (hidden, grad))
    return pl.pallas_call(
        write_out,
        out_shape=(
            jax.ShapeDtypeStruct((TOK, FF_DEV), bf16),
            jax.ShapeDtypeStruct((OUT_ROWS, FF_DEV), jnp.float32),
        ),
        in_specs=[hbm, hbm],
        out_specs=(hbm, hbm),
        scratch_shapes=[dma((2,))],
    )(hidden, grad)


def solution(mesh):
    return jax.shard_map(
        local,
        mesh=mesh,
        in_specs=(P("row", "col"), P(), P(), P(None, "col"), P("col"), P("row", "col"), P("row", "col")),
        out_specs=(P("row", "col"), P("row", "col")),
        check_vma=False,
    )
```
